256 devices in a mesh: row: 16 (over z_hi, y, core), col: 16 (over x, z_lo).
Axes of the slice: x: 4, y: 4, z: 8 (z_hi: 2, z_lo: 4; z = z_hi * 4 + z_lo), core: 2. Of those that a mesh axis runs over, the one named last changes fastest.
Arguments:
- test_grads: bfloat16 [1024, 16384], P('col', 'row'), may hold values from -6 to 6
- inverse_gram: float32 [16384, 16384], P('row', 'col'), may hold values from -0.046875 to 0.046875
- train_grads: bfloat16 [12288, 16384], P('row', 'col'), may hold values from -0.046875 to 0.046875
Outputs:
- scores: float32 [1024, 12288], P('col', 'row')
The draws below stay inside these ranges and needn't reach their ends.
All inputs are finite; a program needn't handle non-finite values.
Results may differ from the reference program's by a relative error of at most 0.0029.
Values may be sent and summed in bfloat16 or wider, within the bound.
No kernel may reach another device: no remote copies, remote signals or barrier semaphores. Data moves between devices by JAX's collectives and lax.ppermute only.
A program may use at most 64 MiB of HBM per device.

```python
import jax
import jax.numpy as jnp
from jax import lax

K = 16384
TESTS = 1024
TRAIN = 12288


def steps_of(key, dims, split, low, top_value):
    def one(axis_at, blocks):
        draws = jax.random.uniform(jax.random.fold_in(jax.random.fold_in(key, 6), axis_at), (blocks,), jnp.float32, low / len(split), top_value / len(split))
        return jnp.repeat(jnp.exp(draws), dims[axis_at] // blocks).reshape((-1,) + (1,) * (len(dims) - axis_at - 1))

    level = one(*split[0])
    for cut in split[1:]:
        level = level * one(*cut)
    return level


def bell_draw(rng, extent, deviation, limit, shards=(), held_as=jnp.bfloat16):
    level = steps_of(rng, extent, shards, -0.22, 0.18) if shards else 1.0
    array = jax.random.normal(rng, extent, jnp.float32) * deviation * level
    return jnp.minimum(jnp.maximum(array, -limit), limit).astype(held_as)


def setup_inputs(seed: int = 0) -> dict:
    streams_of = jax.random.split(jax.random.key(seed), 4)
    test_grads = bell_draw(streams_of[0], (TESTS, K), 1.0, 6.0, ((0, 16), (1, 16)))
    inverse_gram = bell_draw(streams_of[1], (K, K), K ** -0.5, 0.046875, ((0, 16), (1, 16)), jnp.float32)
    train_grads = bell_draw(streams_of[2], (TRAIN, K), K ** -0.5, 0.046875, ((0, 16), (1, 16)))
    return dict(test_grads=test_grads, inverse_gram=inverse_gram, train_grads=train_grads)


def reference(test_grads, inverse_gram, train_grads):
    precond = jnp.dot(test_grads.astype(jnp.float32), inverse_gram, precision=lax.Precision.HIGHEST, preferred_element_type=jnp.float32)
    precond_low = precond.astype(jnp.bfloat16)
    return lax.dot_general(precond_low, train_grads, (((1,), (1,)), ((), ())), preferred_element_type=jnp.float32)
```

```python
import jax
import jax.numpy as jnp
from jax import lax
from jax.experimental import pallas as pl
from jax.experimental.pallas import tpu as pltpu
from jax.sharding import PartitionSpec as P

ZH, Y, CORE, X, ZL = 2, 4, 2, 4, 4
SLOTS = X * ZL
BOTH = ("row", "col")
CROSSED = True
F32, F16, BF16 = jnp.float32, jnp.float16, jnp.bfloat16
VMEM = pl.BlockSpec(memory_space=pltpu.VMEM)
PARAMS = pltpu.CompilerParams(vmem_limit_bytes=48 * 2**20)


def pairs(step):
    def index(zh, y, core, x, zl):
        return ((zh * Y + y) * CORE + core) * (X * ZL) + x * ZL + zl

    return [
        (index(zh, y, core, x, zl), index(*step(zh, y, core, x, zl)))
        for zh in range(ZH)
        for y in range(Y)
        for core in range(CORE)
        for x in range(X)
        for zl in range(ZL)
    ]


TO_CORE = pairs(lambda zh, y, c, x, zl: (zh, y, 1 - c, x, zl))
TO_ZH = pairs(lambda zh, y, c, x, zl: (1 - zh, y, c, x, zl))
TO_Y = [pairs(lambda zh, y, c, x, zl, k=k: (zh, y ^ k, c, x, zl)) for k in range(Y)]
TO_X = [pairs(lambda zh, y, c, x, zl, k=k: (zh, y, c, x ^ k, zl)) for k in range(X)]
TO_ZL = [pairs(lambda zh, y, c, x, zl, k=k: (zh, y, c, x, zl ^ k)) for k in range(ZL)]


def crossed(first):
    def step(zh, y, c, x, zl, k):
        along_x = CROSSED and first == (c == 1) or not CROSSED and not first
        return (zh, y, c, x ^ k, zl) if along_x else (zh, y, c, x, zl ^ k)

    return [pairs(lambda *at, k=k: step(*at, k)) for k in range(4)]


FIRST, SECOND = crossed(True), crossed(False)


def send(value, perm):
    return lax.ppermute(value, BOTH, perm)


def gather(block, perms):
    return jnp.stack([block] + [send(block, perm) for perm in perms[1:]])


def exponent(bound):
    return jnp.clip(15.0 - jnp.ceil(jnp.log2(bound)), -100.0, 100.0)


def pack(values, e):
    head = (values * jnp.exp2(e)).astype(F16)
    return jnp.concatenate([head, jnp.full((8, values.shape[1]), e, F16)])


def unpack(packed):
    e = packed[-1, 0].astype(F32)
    return packed[:-8].astype(F32) * jnp.exp2(-e), e


def scatter_sum(blocks, perms, e):
    total, bound = blocks[0], jnp.exp2(-e)
    for block, perm in zip(blocks[1:], perms[1:]):
        got, its = unpack(send(pack(block, e), perm))
        total, bound = total + got, bound + jnp.exp2(-its)
    return total, -jnp.ceil(jnp.log2(bound))


def split(g):
    high = lax.reduce_precision(g, 8, 7)
    return high.astype(BF16), (g - high).astype(BF16)


def place():
    row = lax.axis_index("row")
    return row % CORE, (row // CORE) % Y


def precond_kernel(tests, near_high, near_low, far_high, far_low, out, top):
    core, y = place()
    rows, width = tests.shape[0], near_high.shape[0]
    group = rows // (SLOTS * Y)
    step = 256

    def body(i, most):
        at = pl.ds(pl.multiple_of(i * step, step), step)
        acc = jnp.dot(tests[:, :width], near_high[:, at], preferred_element_type=F32)
        acc += jnp.dot(tests[:, :width], near_low[:, at], preferred_element_type=F32)
        acc += jnp.dot(tests[:, width:], far_high[:, at], preferred_element_type=F32)
        acc += jnp.dot(tests[:, width:], far_low[:, at], preferred_element_type=F32)
        parts = acc.reshape(4, 4, Y, group, step)
        for second in range(4):
            for first in range(4):
                slot = second * 4 + first
                if CROSSED:
                    slot = jnp.where(core == 0, slot, first * 4 + second)
                for quarter in range(Y):
                    out[quarter ^ y, slot, :, at] = parts[second, first, quarter]
        return jnp.maximum(most, jnp.max(jnp.abs(acc)))

    most = lax.fori_loop(0, near_high.shape[1] // step, body, jnp.float32(0))
    top[...] = jnp.full(top.shape, most)


def scores_kernel(low, near, far, out, top):
    _, y = place()
    group = low.shape[1] // SLOTS
    step = 256
    steps = near.shape[0] // step
    tests = low[...].reshape(-1, low.shape[2])
    most = jnp.float32(0)
    for at_out, trains in ((0, near), (near.shape[0], far)):

        def body(i, most, at_out=at_out, trains=trains):
            rows = pl.ds(pl.multiple_of(i * step, step), step)
            at = pl.ds(pl.multiple_of(at_out + i * step, step), step)
            acc = lax.dot_general(
                tests, trains[rows, :], (((1,), (1,)), ((), ())), preferred_element_type=F32
            )
            parts = acc.reshape(Y, SLOTS, group, step)
            for k in range(Y):
                out[:, k ^ y, :, at] = parts[k]
            return jnp.maximum(most, jnp.max(jnp.abs(acc)))

        most = lax.fori_loop(0, steps, body, most)
    top[...] = jnp.full(top.shape, most)


def call(kernel, shape, args, flops):
    top = jax.ShapeDtypeStruct((8, 128), F32)
    out, top = pl.pallas_call(
        kernel,
        out_shape=(jax.ShapeDtypeStruct(shape, F32), top),
        in_specs=[VMEM] * len(args),
        out_specs=(VMEM, VMEM),
        compiler_params=PARAMS,
        cost_estimate=pl.CostEstimate(flops=flops, bytes_accessed=8 * 2**20, transcendentals=0),
    )(*args)
    return out, exponent(top[0, 0])


def per_device(test_grads, inverse_gram, train_grads):
    core, _ = place()
    tests, width = test_grads.shape
    trains = train_grads.shape[0]
    half = tests // 2
    group = half // Y
    depth = inverse_gram.shape[1]

    mine = jnp.where(core == 0, test_grads[:half], test_grads[half:])
    other = jnp.where(core == 0, test_grads[half:], test_grads[:half])
    block = jnp.concatenate([mine, send(other, TO_CORE)], axis=1)

    near_gram = split(inverse_gram)
    far_gram = split(send(inverse_gram, TO_CORE))
    far_trains = send(train_grads, TO_CORE)

    block = gather(block, FIRST).reshape(4 * half, 2 * width)
    every = gather(block, SECOND).reshape(SLOTS * half, 2 * width)

    part, e = call(
        precond_kernel,
        (Y, SLOTS, group, depth),
        (every, *near_gram, *far_gram),
        8 * SLOTS * half * width * depth,
    )
    part = part.reshape(Y, SLOTS * group, depth)
    total, e = scatter_sum([part[k] for k in range(Y)], TO_Y, e)
    total = total + unpack(send(pack(total, e), TO_ZH))[0]
    low = gather(total.astype(BF16), TO_Y)

    scores, e = call(
        scores_kernel,
        (SLOTS, Y, group, 2 * trains),
        (low, train_grads, far_trains),
        4 * SLOTS * half * trains * depth,
    )
    scores = scores.reshape(X, ZL * half, 2 * trains)
    scores, e = scatter_sum([scores[k] for k in range(X)], TO_X, e)
    scores = scores.reshape(ZL, half, 2 * trains)
    scores, e = scatter_sum([scores[k] for k in range(ZL)], TO_ZL, e)

    kept, sent = scores[:, :trains], scores[:, trains:]
    got = send(sent, TO_CORE)
    return jnp.where(
        core == 0, jnp.concatenate([kept, got]), jnp.concatenate([got, kept])
    )


def solution(mesh):
    placed = (P("col", "row"), P("row", "col"), P("row", "col"))
    return jax.shard_map(
        per_device, mesh=mesh, in_specs=placed, out_specs=P("col", "row"), check_vma=False
    )
```

```python
import jax
import jax.numpy as jnp
from jax import lax
from jax.experimental import pallas as pl
from jax.experimental.pallas import tpu as pltpu
from jax.sharding import PartitionSpec as P

ZH, Y, CORE, X, ZL = 2, 4, 2, 4, 4
BOTH = ("row", "col")
F32, F16, BF16 = jnp.float32, jnp.float16, jnp.bfloat16
VMEM = pl.BlockSpec(memory_space=pltpu.VMEM)
PARAMS = pltpu.CompilerParams(vmem_limit_bytes=24 * 2**20)


def pairs(step):
    def index(zh, y, core, x, zl):
        return ((zh * Y + y) * CORE + core) * (X * ZL) + x * ZL + zl

    return [
        (index(zh, y, core, x, zl), index(*step(zh, y, core, x, zl)))
        for zh in range(ZH)
        for y in range(Y)
        for core in range(CORE)
        for x in range(X)
        for zl in range(ZL)
    ]


TO_CORE = pairs(lambda zh, y, c, x, zl: (zh, y, 1 - c, x, zl))
TO_ZH = pairs(lambda zh, y, c, x, zl: (1 - zh, y, c, x, zl))
TO_Y = [pairs(lambda zh, y, c, x, zl, k=k: (zh, y ^ k, c, x, zl)) for k in range(Y)]


def crossed(first):
    def step(zh, y, c, x, zl, k):
        along_x = first == (c == 1)
        return (zh, y, c, x ^ k, zl) if along_x else (zh, y, c, x, zl ^ k)

    return [pairs(lambda *at, k=k: step(*at, k)) for k in range(4)]


FIRST, SECOND = crossed(True), crossed(False)


def send(value, perm):
    return lax.ppermute(value, BOTH, perm)


def gather(block, perms):
    return jnp.stack([block] + [send(block, perm) for perm in perms[1:]])


def pack(values, e):
    head = (values * jnp.exp2(e)).astype(F16)
    tail = jnp.broadcast_to(e, (8, values.shape[1])).astype(F16)
    return jnp.concatenate([head, tail])


def unpack(packed):
    e = packed[-1:].astype(F32)
    return packed[:-8].astype(F32) * jnp.exp2(-e), e


def scatter_sum(blocks, perms, e):
    total, least = blocks[0], e
    sent = [send(pack(block, e), perm) for block, perm in zip(blocks[1:], perms[1:])]
    for packed in sent:
        got, its = unpack(packed)
        total, least = total + got, jnp.minimum(least, its)
    return total, least - 2.0


def y_place():
    return (lax.axis_index("row") // CORE) % Y


def note_top(i, acc, most, top):
    @pl.when(i == 0)
    def _():
        most[...] = jnp.zeros(most.shape, F32)

    most[...] = jnp.maximum(most[...], jnp.max(jnp.abs(acc).reshape(-1, 8, acc.shape[1]), axis=0))

    @pl.when(i == pl.num_programs(0) - 1)
    def _():
        bound = jnp.broadcast_to(jnp.max(most[...]), top.shape)
        top[...] = jnp.clip(15.0 - jnp.ceil(jnp.log2(bound)), -100.0, 100.0)


def precond_kernel(tests, near, far, out, top, most):
    i, y = pl.program_id(0), y_place()
    rows, width = tests.shape[0], near.shape[0]
    acc = None
    for at, gram in ((0, near), (width, far)):
        high = gram[...].astype(BF16)
        low = (gram[...] - high.astype(F32)).astype(BF16)
        for part in (high, low):
            new = jnp.dot(tests[:, at : at + width], part, preferred_element_type=F32)
            acc = new if acc is None else acc + new
    parts = acc.reshape(out.shape[1], Y, out.shape[2], -1)
    for quarter in range(Y):
        out[quarter ^ y] = parts[:, quarter]
    note_top(i, acc, most, top)


def scores_kernel(low, near, far, out, top, most):
    i, y = pl.program_id(0), y_place()
    tests = low[...].reshape(-1, low.shape[2])

    def product(trains):
        acc = lax.dot_general(
            tests, trains[...], (((1,), (1,)), ((), ())), preferred_element_type=F32
        )
        parts = acc.reshape(Y, out.shape[0], out.shape[2], -1)
        for k in range(Y):
            out[:, k ^ y] = parts[k]
        note_top(i, acc, most, top)

    pl.when(i < pl.num_programs(0) // 2)(lambda: product(near))
    pl.when(i >= pl.num_programs(0) // 2)(lambda: product(far))


def precond(tests, near, far):
    rows, (width, depth) = tests.shape[0], near.shape
    slots, group, step = rows // 32, 8, 256
    block = pl.BlockSpec((width, step), lambda i: (0, i))
    return pl.pallas_call(
        precond_kernel,
        grid=(depth // step,),
        in_specs=[VMEM, block, block],
        out_specs=(pl.BlockSpec((Y, slots, group, step), lambda i: (0, 0, 0, i)), pl.BlockSpec((8, depth), lambda i: (0, 0))),
        out_shape=(jax.ShapeDtypeStruct((Y, slots, group, depth), F32), jax.ShapeDtypeStruct((8, depth), F32)),
        scratch_shapes=[pltpu.VMEM((8, step), F32)],
        compiler_params=PARAMS,
        cost_estimate=pl.CostEstimate(flops=8 * rows * width * depth, bytes_accessed=2**23, transcendentals=0),
        name="precond",
    )(tests, near, far)


def scores_of(low, near, far):
    trains, depth = near.shape
    slots, group, step = low.shape[1] // 8, 8, 256
    n = trains // step
    return pl.pallas_call(
        scores_kernel,
        grid=(2 * n,),
        in_specs=[
            VMEM,
            pl.BlockSpec((step, depth), lambda i: (jnp.minimum(i, n - 1), 0)),
            pl.BlockSpec((step, depth), lambda i: (jnp.maximum(i - n, 0), 0)),
        ],
        out_specs=(pl.BlockSpec((slots, Y, group, step), lambda i: (0, 0, 0, i)), pl.BlockSpec((8, 2 * trains), lambda i: (0, 0))),
        out_shape=(jax.ShapeDtypeStruct((slots, Y, group, 2 * trains), F32), jax.ShapeDtypeStruct((8, 2 * trains), F32)),
        scratch_shapes=[pltpu.VMEM((8, step), F32)],
        compiler_params=PARAMS,
        cost_estimate=pl.CostEstimate(flops=4 * low.shape[0] * low.shape[1] * trains * depth, bytes_accessed=2**22, transcendentals=0),
        name="scores",
    )(low, near, far)


def per_device(test_grads, inverse_gram, train_grads):
    core = lax.axis_index("row") % CORE
    tests, width = test_grads.shape
    trains = train_grads.shape[0]
    half = tests // 2

    mine = jnp.where(core == 0, test_grads[:half], test_grads[half:])
    other = jnp.where(core == 0, test_grads[half:], test_grads[:half])
    got = send(other, TO_CORE)
    got, inverse_gram, train_grads = lax.optimization_barrier((got, inverse_gram, train_grads))
    far_gram = send(inverse_gram, TO_CORE)
    far_trains = send(train_grads, TO_CORE)

    block = jnp.concatenate([mine, got], axis=1)
    block = gather(block, FIRST).reshape(4 * half, 2 * width)
    slot1, slot3 = send(block, SECOND[1]), send(block, SECOND[3])
    part = precond(jnp.concatenate([block, slot1]), inverse_gram, far_gram)
    slot3, part = lax.optimization_barrier((slot3, part))
    slot2 = send(slot3, SECOND[1])

    def summed(part, e):
        part = part.reshape(Y, -1, part.shape[3])
        return scatter_sum([part[k] for k in range(Y)], TO_Y, e[:1])

    def rounded(total, e):
        return (total + unpack(send(pack(total, e), TO_ZH))[0]).astype(BF16)

    def product(low):
        scores, e = scores_of(low, train_grads, far_trains)
        scores = scores.reshape(2, 4 * half, 2 * trains)
        return [(scores[j], e[:1]) for j in range(2)]

    first = summed(*part)
    part = precond(jnp.concatenate([slot2, slot3]), inverse_gram, far_gram)
    first, part = lax.optimization_barrier((first, part))
    second = summed(*part)
    low0 = rounded(*first)
    low1 = rounded(*second)
    low0 = gather(low0, TO_Y)
    low1 = gather(low1, TO_Y)
    block0, block1 = product(low0)
    block2, block3 = product(low1)
    total, least = block0
    for (block, e), k in ((block1, 1), (block2, 2), (block3, 3)):
        got, its = unpack(send(pack(block, e), SECOND[k]))
        total, least = total + got, jnp.minimum(least, its)
    total = total.reshape(4, half, 2 * trains)
    total, _ = scatter_sum([total[k] for k in range(4)], FIRST, least - 2.0)

    kept, sent = total[:, :trains], total[:, trains:]
    got = send(sent, TO_CORE)
    return jnp.where(
        core == 0, jnp.concatenate([kept, got]), jnp.concatenate([got, kept])
    )


def solution(mesh):
    placed = (P("col", "row"), P("row", "col"), P("row", "col"))
    return jax.shard_map(
        per_device, mesh=mesh, in_specs=placed, out_specs=P("col", "row"), check_vma=False
    )
```

```python
import jax
import jax.numpy as jnp
from jax import lax
from jax.experimental import pallas as pl
from jax.experimental.pallas import tpu as pltpu
from jax.sharding import PartitionSpec as P

ZH, Y, CORE, X, ZL = 2, 4, 2, 4, 4
BOTH = ("row", "col")
F32, F16, BF16 = jnp.float32, jnp.float16, jnp.bfloat16
VMEM = pl.BlockSpec(memory_space=pltpu.VMEM)
PARAMS = pltpu.CompilerParams(vmem_limit_bytes=24 * 2**20)


def pairs(step):
    def index(zh, y, core, x, zl):
        return ((zh * Y + y) * CORE + core) * (X * ZL) + x * ZL + zl

    return [
        (index(zh, y, core, x, zl), index(*step(zh, y, core, x, zl)))
        for zh in range(ZH)
        for y in range(Y)
        for core in range(CORE)
        for x in range(X)
        for zl in range(ZL)
    ]


TO_CORE = pairs(lambda zh, y, c, x, zl: (zh, y, 1 - c, x, zl))
TO_ZH = pairs(lambda zh, y, c, x, zl: (1 - zh, y, c, x, zl))
TO_Y = [pairs(lambda zh, y, c, x, zl, k=k: (zh, y ^ k, c, x, zl)) for k in range(Y)]


def crossed(first):
    def step(zh, y, c, x, zl, k):
        along_x = first == (c == 1)
        return (zh, y, c, x ^ k, zl) if along_x else (zh, y, c, x, zl ^ k)

    return [pairs(lambda *at, k=k: step(*at, k)) for k in range(4)]


FIRST, SECOND = crossed(True), crossed(False)


def send(value, perm):
    return lax.ppermute(value, BOTH, perm)


def gather(block, perms):
    return jnp.stack([block] + [send(block, perm) for perm in perms[1:]])


def pack(values, e):
    head = (values * jnp.exp2(e)).astype(F16)
    tail = jnp.broadcast_to(e, (8, values.shape[1])).astype(F16)
    return jnp.concatenate([head, tail])


def unpack(packed):
    e = packed[-1:].astype(F32)
    return packed[:-8].astype(F32) * jnp.exp2(-e), e


def scatter_sum(blocks, perms, e):
    total, least = blocks[0], e
    sent = [send(pack(block, e), perm) for block, perm in zip(blocks[1:], perms[1:])]
    for packed in sent:
        got, its = unpack(packed)
        total, least = total + got, jnp.minimum(least, its)
    return total, least - 2.0


def y_place():
    return (lax.axis_index("row") // CORE) % Y


def exponent_of(most, top):
    bound = jnp.broadcast_to(jnp.max(most), top.shape)
    top[...] = jnp.clip(15.0 - jnp.ceil(jnp.log2(bound)), -100.0, 100.0)


def largest(most, acc):
    new = jnp.max(jnp.abs(acc).reshape(-1, 8, acc.shape[1]), axis=0)
    return new if most is None else jnp.maximum(most, new)


def precond_kernel(tests, near, far, out, top):
    y, width, step = y_place(), near.shape[0], 512
    most = None
    for i in range(0, near.shape[1], step):
        acc = None
        for at, gram in ((0, near), (width, far)):
            gram = gram[:, i : i + step]
            high = gram.astype(BF16)
            low = (gram - high.astype(F32)).astype(BF16)
            for part in (high, low):
                new = jnp.dot(tests[:, at : at + width], part, preferred_element_type=F32)
                acc = new if acc is None else acc + new
        parts = acc.reshape(out.shape[1], Y, out.shape[2], step)
        for quarter in range(Y):
            out[quarter ^ y, :, :, i : i + step] = parts[:, quarter]
        most = largest(most, acc)
    exponent_of(most, top)


def scores_kernel(low, near, far, out, top):
    y, trains = y_place(), near.shape[0]
    tests = low[...].reshape(-1, low.shape[2])
    most = None
    for at, block in ((0, near), (trains, far)):
        acc = lax.dot_general(
            tests, block[...], (((1,), (1,)), ((), ())), preferred_element_type=F32
        )
        parts = acc.reshape(Y, out.shape[0], out.shape[2], trains)
        for k in range(Y):
            out[:, k ^ y, :, at : at + trains] = parts[k]
        most = largest(most, acc)
    exponent_of(most, top)


def precond(tests, near, far):
    rows, (width, depth) = tests.shape[0], near.shape
    return pl.pallas_call(
        precond_kernel,
        in_specs=[VMEM] * 3,
        out_specs=(VMEM, VMEM),
        out_shape=(
            jax.ShapeDtypeStruct((Y, rows // 32, 8, depth), F32),
            jax.ShapeDtypeStruct((8, depth), F32),
        ),
        compiler_params=PARAMS,
        cost_estimate=pl.CostEstimate(
            flops=8 * rows * width * depth, bytes_accessed=2**23, transcendentals=0
        ),
        name="precond",
    )(tests, near, far)


def scores_of(low, near, far):
    trains, depth = near.shape
    return pl.pallas_call(
        scores_kernel,
        in_specs=[VMEM] * 3,
        out_specs=(VMEM, VMEM),
        out_shape=(
            jax.ShapeDtypeStruct((low.shape[1] // 8, Y, 8, 2 * trains), F32),
            jax.ShapeDtypeStruct((8, 2 * trains), F32),
        ),
        compiler_params=PARAMS,
        cost_estimate=pl.CostEstimate(
            flops=4 * low.shape[0] * low.shape[1] * trains * depth,
            bytes_accessed=2**22,
            transcendentals=0,
        ),
        name="scores",
    )(low, near, far)


def near_kernel(gram, out, sem):
    copy = pltpu.make_async_copy(gram, out, sem)
    copy.start()
    copy.wait()


def brought_in(gram):
    return pl.pallas_call(
        near_kernel,
        in_specs=[pl.BlockSpec(memory_space=pl.ANY)],
        out_specs=VMEM,
        out_shape=jax.ShapeDtypeStruct(gram.shape, F32),
        scratch_shapes=[pltpu.SemaphoreType.DMA],
        compiler_params=PARAMS,
        name="brought_in",
    )(gram)


def per_device(test_grads, inverse_gram, train_grads):
    core = lax.axis_index("row") % CORE
    tests, width = test_grads.shape
    trains = train_grads.shape[0]
    half = tests // 2

    mine = jnp.where(core == 0, test_grads[:half], test_grads[half:])
    other = jnp.where(core == 0, test_grads[half:], test_grads[:half])
    got = send(other, TO_CORE)
    got, inverse_gram, train_grads = lax.optimization_barrier((got, inverse_gram, train_grads))
    far_gram = send(inverse_gram, TO_CORE)
    far_trains = send(train_grads, TO_CORE)

    block = jnp.concatenate([mine, got], axis=1)
    block = gather(block, FIRST).reshape(4 * half, 2 * width)
    near = brought_in(inverse_gram)
    block, near = lax.optimization_barrier((block, near))
    slot1, slot3 = send(block, SECOND[1]), send(block, SECOND[3])
    part = precond(jnp.concatenate([block, slot1]), near, far_gram)
    slot3, part = lax.optimization_barrier((slot3, part))
    slot2 = send(slot3, SECOND[1])

    def summed(part, e):
        part = part.reshape(Y, -1, part.shape[3])
        return scatter_sum([part[k] for k in range(Y)], TO_Y, e[:1])

    def rounded(total, e):
        return (total + unpack(send(pack(total, e), TO_ZH))[0]).astype(BF16)

    def product(low):
        scores, e = scores_of(low, train_grads, far_trains)
        scores = scores.reshape(2, 4 * half, 2 * trains)
        return [(scores[j], e[:1]) for j in range(2)]

    first = summed(*part)
    part = precond(jnp.concatenate([slot2, slot3]), near, far_gram)
    first, part = lax.optimization_barrier((first, part))
    second = summed(*part)
    low0 = rounded(*first)
    low1 = rounded(*second)
    low0 = gather(low0, TO_Y)
    low1 = gather(low1, TO_Y)
    block0, block1 = product(low0)
    block2, block3 = product(low1)
    total, least = block0
    for (block, e), k in ((block1, 1), (block2, 2), (block3, 3)):
        got, its = unpack(send(pack(block, e), SECOND[k]))
        total, least = total + got, jnp.minimum(least, its)
    total = total.reshape(4, half, 2 * trains)
    total, _ = scatter_sum([total[k] for k in range(4)], FIRST, least - 2.0)

    kept, sent = total[:, :trains], total[:, trains:]
    got = send(sent, TO_CORE)
    return jnp.where(
        core == 0, jnp.concatenate([kept, got]), jnp.concatenate([got, kept])
    )


def solution(mesh):
    placed = (P("col", "row"), P("row", "col"), P("row", "col"))
    return jax.shard_map(
        per_device, mesh=mesh, in_specs=placed, out_specs=P("col", "row"), check_vma=False
    )
```

```python
import jax
import jax.numpy as jnp
from jax import lax
from jax.experimental import pallas as pl
from jax.experimental.pallas import tpu as pltpu
from jax.sharding import PartitionSpec as P

ZH, Y, CORE, X, ZL = 2, 4, 2, 4, 4
BOTH = ("row", "col")
F32, F16, BF16 = jnp.float32, jnp.float16, jnp.bfloat16
VMEM = pl.BlockSpec(memory_space=pltpu.VMEM)
PARAMS = pltpu.CompilerParams(vmem_limit_bytes=24 * 2**20)


def pairs(step):
    def index(zh, y, core, x, zl):
        return ((zh * Y + y) * CORE + core) * (X * ZL) + x * ZL + zl

    return [
        (index(zh, y, core, x, zl), index(*step(zh, y, core, x, zl)))
        for zh in range(ZH)
        for y in range(Y)
        for core in range(CORE)
        for x in range(X)
        for zl in range(ZL)
    ]


TO_CORE = pairs(lambda zh, y, c, x, zl: (zh, y, 1 - c, x, zl))
TO_ZH = pairs(lambda zh, y, c, x, zl: (1 - zh, y, c, x, zl))
TO_Y = [pairs(lambda zh, y, c, x, zl, k=k: (zh, y ^ k, c, x, zl)) for k in range(Y)]


def crossed(first):
    def step(zh, y, c, x, zl, k):
        along_x = first == (c == 1)
        return (zh, y, c, x ^ k, zl) if along_x else (zh, y, c, x, zl ^ k)

    return [pairs(lambda *at, k=k: step(*at, k)) for k in range(4)]


FIRST, SECOND = crossed(True), crossed(False)


def send(value, perm):
    return lax.ppermute(value, BOTH, perm)


def gather(block, perms):
    return jnp.stack([block] + [send(block, perm) for perm in perms[1:]])


def pack(values, e):
    head = (values * jnp.exp2(e)).astype(F16)
    tail = jnp.broadcast_to(e, (8, values.shape[1])).astype(F16)
    return jnp.concatenate([head, tail])


def unpack(packed):
    e = packed[-1:].astype(F32)
    return packed[:-8].astype(F32) * jnp.exp2(-e), e


def scatter_sum(blocks, perms, e, order=(1, 2, 3)):
    total, least = blocks[0], e
    sent = [send(pack(blocks[k], e), perms[k]) for k in order]
    for packed in sent:
        got, its = unpack(packed)
        total, least = total + got, jnp.minimum(least, its)
    return total, least - 2.0


def y_place():
    return (lax.axis_index("row") // CORE) % Y


def exponent_of(most, top):
    bound = jnp.broadcast_to(jnp.max(most), top.shape)
    top[...] = jnp.clip(15.0 - jnp.ceil(jnp.log2(bound)), -100.0, 100.0)


def largest(most, acc):
    new = jnp.max(jnp.abs(acc).reshape(-1, 8, acc.shape[1]), axis=0)
    return new if most is None else jnp.maximum(most, new)


def precond_kernel(tests, near, far, out, top):
    y, width, step = y_place(), near.shape[0], 512
    most = None
    for i in range(0, near.shape[1], step):
        acc = None
        for at, gram in ((0, near), (width, far)):
            gram = gram[:, i : i + step]
            high = gram.astype(BF16)
            low = (gram - high.astype(F32)).astype(BF16)
            for part in (high, low):
                new = jnp.dot(tests[:, at : at + width], part, preferred_element_type=F32)
                acc = new if acc is None else acc + new
        parts = acc.reshape(out.shape[1], Y, out.shape[2], step)
        for quarter in range(Y):
            out[quarter ^ y, :, :, i : i + step] = parts[:, quarter]
        most = largest(most, acc)
    exponent_of(most, top)


def scores_kernel(low, near, far, out, top):
    y, trains = y_place(), near.shape[0]
    tests = low[...].reshape(-1, low.shape[2])
    most = None
    for at, block in ((0, near), (trains, far)):
        acc = lax.dot_general(
            tests, block[...], (((1,), (1,)), ((), ())), preferred_element_type=F32
        )
        parts = acc.reshape(Y, out.shape[0], out.shape[2], trains)
        for k in range(Y):
            out[:, k ^ y, :, at : at + trains] = parts[k]
        most = largest(most, acc)
    exponent_of(most, top)


def precond(tests, near, far):
    rows, (width, depth) = tests.shape[0], near.shape
    return pl.pallas_call(
        precond_kernel,
        in_specs=[VMEM] * 3,
        out_specs=(VMEM, VMEM),
        out_shape=(
            jax.ShapeDtypeStruct((Y, rows // 32, 8, depth), F32),
            jax.ShapeDtypeStruct((8, depth), F32),
        ),
        compiler_params=PARAMS,
        cost_estimate=pl.CostEstimate(
            flops=8 * rows * width * depth, bytes_accessed=2**23, transcendentals=0
        ),
        name="precond",
    )(tests, near, far)


def scores_of(low, near, far):
    trains, depth = near.shape
    return pl.pallas_call(
        scores_kernel,
        in_specs=[VMEM] * 3,
        out_specs=(VMEM, VMEM),
        out_shape=(
            jax.ShapeDtypeStruct((low.shape[1] // 8, Y, 8, 2 * trains), F32),
            jax.ShapeDtypeStruct((8, 2 * trains), F32),
        ),
        compiler_params=PARAMS,
        cost_estimate=pl.CostEstimate(
            flops=4 * low.shape[0] * low.shape[1] * trains * depth,
            bytes_accessed=2**22,
            transcendentals=0,
        ),
        name="scores",
    )(low, near, far)


def near_kernel(gram, out, sem):
    copy = pltpu.make_async_copy(gram, out, sem)
    copy.start()
    copy.wait()


def brought_in(gram):
    return pl.pallas_call(
        near_kernel,
        in_specs=[pl.BlockSpec(memory_space=pl.ANY)],
        out_specs=VMEM,
        out_shape=jax.ShapeDtypeStruct(gram.shape, F32),
        scratch_shapes=[pltpu.SemaphoreType.DMA],
        compiler_params=PARAMS,
        name="brought_in",
    )(gram)


def per_device(test_grads, inverse_gram, train_grads):
    core = lax.axis_index("row") % CORE
    tests, width = test_grads.shape
    trains = train_grads.shape[0]
    half = tests // 2

    mine = jnp.where(core == 0, test_grads[:half], test_grads[half:])
    other = jnp.where(core == 0, test_grads[half:], test_grads[:half])
    got = send(other, TO_CORE)
    got, inverse_gram, train_grads = lax.optimization_barrier((got, inverse_gram, train_grads))
    far_gram = send(inverse_gram, TO_CORE)
    far_trains = send(train_grads, TO_CORE)

    block = jnp.concatenate([mine, got], axis=1)
    block = gather(block, FIRST).reshape(4 * half, 2 * width)
    near = brought_in(inverse_gram)
    block, near = lax.optimization_barrier((block, near))
    slot1, slot3 = send(block, SECOND[1]), send(block, SECOND[3])
    part = precond(jnp.concatenate([block, slot1]), near, far_gram)
    slot3, part = lax.optimization_barrier((slot3, part))
    slot2 = send(slot3, SECOND[1])

    def summed(part, e):
        part = part.reshape(Y, -1, part.shape[3])
        return scatter_sum([part[k] for k in range(Y)], TO_Y, e[:1])

    def rounded(total, e):
        return (total + unpack(send(pack(total, e), TO_ZH))[0]).astype(BF16)

    def product(low):
        scores, e = scores_of(low, train_grads, far_trains)
        scores = scores.reshape(2, 4 * half, 2 * trains)
        return [(scores[j], e[:1]) for j in range(2)]

    first = summed(*part)
    part = precond(jnp.concatenate([slot2, slot3]), near, far_gram)
    first, part = lax.optimization_barrier((first, part))
    second = summed(*part)
    low0 = rounded(*first)
    low1 = rounded(*second)
    low0 = gather(low0, TO_Y)
    low1 = gather(low1, TO_Y)
    block0, block1 = product(low0)
    block2, block3 = product(low1)
    total, least = block0
    for (block, e), k in ((block1, 1), (block3, 3), (block2, 2)):
        got, its = unpack(send(pack(block, e), SECOND[k]))
        total, least = total + got, jnp.minimum(least, its)
    total = total.reshape(4, half, 2 * trains)
    total, _ = scatter_sum([total[k] for k in range(4)], FIRST, least - 2.0, (3, 2, 1))

    kept, sent = total[:, :trains], total[:, trains:]
    got = send(sent, TO_CORE)
    return jnp.where(
        core == 0, jnp.concatenate([kept, got]), jnp.concatenate([got, kept])
    )


def solution(mesh):
    placed = (P("col", "row"), P("row", "col"), P("row", "col"))
    return jax.shard_map(
        per_device, mesh=mesh, in_specs=placed, out_specs=P("col", "row"), check_vma=False
    )
```

```python
import jax
import jax.numpy as jnp
from jax import lax
from jax.experimental import pallas as pl
from jax.experimental.pallas import tpu as pltpu
from jax.sharding import PartitionSpec as P

ZH, Y, CORE, X, ZL = 2, 4, 2, 4, 4
BOTH = ("row", "col")
F32, F16, BF16 = jnp.float32, jnp.float16, jnp.bfloat16
VMEM = pl.BlockSpec(memory_space=pltpu.VMEM)
PARAMS = pltpu.CompilerParams(vmem_limit_bytes=24 * 2**20)


def pairs(step):
    def index(zh, y, core, x, zl):
        return ((zh * Y + y) * CORE + core) * (X * ZL) + x * ZL + zl

    return [
        (index(zh, y, core, x, zl), index(*step(zh, y, core, x, zl)))
        for zh in range(ZH)
        for y in range(Y)
        for core in range(CORE)
        for x in range(X)
        for zl in range(ZL)
    ]


TO_CORE = pairs(lambda zh, y, c, x, zl: (zh, y, 1 - c, x, zl))
TO_ZH = pairs(lambda zh, y, c, x, zl: (1 - zh, y, c, x, zl))
TO_Y = [pairs(lambda zh, y, c, x, zl, k=k: (zh, y ^ k, c, x, zl)) for k in range(Y)]


def crossed(first):
    def step(zh, y, c, x, zl, k):
        along_x = first == (c == 1)
        return (zh, y, c, x ^ k, zl) if along_x else (zh, y, c, x, zl ^ k)

    return [pairs(lambda *at, k=k: step(*at, k)) for k in range(4)]


FIRST, SECOND = crossed(True), crossed(False)


def send(value, perm):
    return lax.ppermute(value, BOTH, perm)


def gather(block, perms):
    return jnp.stack([block] + [send(block, perm) for perm in perms[1:]])


def pack(values, e):
    head = (values * jnp.exp2(e)).astype(F16)
    tail = jnp.broadcast_to(e, (8, values.shape[1])).astype(F16)
    return jnp.concatenate([head, tail])


def unpack(packed):
    e = packed[-1:].astype(F32)
    return packed[:-8].astype(F32) * jnp.exp2(-e), e


def scatter_sum(blocks, perms, e, order=(1, 2, 3)):
    total, least = blocks[0], e
    sent = [send(pack(blocks[k], e), perms[k]) for k in order]
    for packed in sent:
        got, its = unpack(packed)
        total, least = total + got, jnp.minimum(least, its)
    return total, least - 2.0


def y_place():
    return (lax.axis_index("row") // CORE) % Y


def exponent_of(most, top):
    bound = jnp.broadcast_to(jnp.max(most), top.shape)
    top[...] = jnp.clip(15.0 - jnp.ceil(jnp.log2(bound)), -100.0, 100.0)


def largest(most, acc):
    new = jnp.max(jnp.abs(acc).reshape(-1, 8, acc.shape[1]), axis=0)
    return new if most is None else jnp.maximum(most, new)


def precond_kernel(tests, near, far, out, top):
    y, width, step = y_place(), near.shape[0], 512
    most = None
    for i in range(0, near.shape[1], step):
        acc = None
        for at, gram in ((0, near), (width, far)):
            gram = gram[:, i : i + step]
            high = gram.astype(BF16)
            low = (gram - high.astype(F32)).astype(BF16)
            for part in (high, low):
                new = jnp.dot(tests[:, at : at + width], part, preferred_element_type=F32)
                acc = new if acc is None else acc + new
        parts = acc.reshape(out.shape[1], Y, out.shape[2], step)
        for quarter in range(Y):
            out[quarter ^ y, :, :, i : i + step] = parts[:, quarter]
        most = largest(most, acc)
    exponent_of(most, top)


def scores_kernel(low, near, far, out, top):
    y, trains = y_place(), near.shape[0]
    tests = low[...].reshape(-1, low.shape[2])
    most = None
    for at, block in ((0, near), (trains, far)):
        acc = lax.dot_general(
            tests, block[...], (((1,), (1,)), ((), ())), preferred_element_type=F32
        )
        parts = acc.reshape(Y, out.shape[0], out.shape[2], trains)
        for k in range(Y):
            out[:, k ^ y, :, at : at + trains] = parts[k]
        most = largest(most, acc)
    exponent_of(most, top)


def precond(tests, near, far):
    rows, (width, depth) = tests.shape[0], near.shape
    return pl.pallas_call(
        precond_kernel,
        in_specs=[VMEM] * 3,
        out_specs=(VMEM, VMEM),
        out_shape=(
            jax.ShapeDtypeStruct((Y, rows // 32, 8, depth), F32),
            jax.ShapeDtypeStruct((8, depth), F32),
        ),
        compiler_params=PARAMS,
        cost_estimate=pl.CostEstimate(
            flops=8 * rows * width * depth, bytes_accessed=2**23, transcendentals=0
        ),
        name="precond",
    )(tests, near, far)


def scores_of(low, near, far):
    trains, depth = near.shape
    return pl.pallas_call(
        scores_kernel,
        in_specs=[VMEM] * 3,
        out_specs=(VMEM, VMEM),
        out_shape=(
            jax.ShapeDtypeStruct((low.shape[1] // 8, Y, 8, 2 * trains), F32),
            jax.ShapeDtypeStruct((8, 2 * trains), F32),
        ),
        compiler_params=PARAMS,
        cost_estimate=pl.CostEstimate(
            flops=4 * low.shape[0] * low.shape[1] * trains * depth,
            bytes_accessed=2**22,
            transcendentals=0,
        ),
        name="scores",
    )(low, near, far)


def near_kernel(gram, out, sem):
    copy = pltpu.make_async_copy(gram, out, sem)
    copy.start()
    copy.wait()


def brought_in(gram):
    return pl.pallas_call(
        near_kernel,
        in_specs=[pl.BlockSpec(memory_space=pl.ANY)],
        out_specs=VMEM,
        out_shape=jax.ShapeDtypeStruct(gram.shape, F32),
        scratch_shapes=[pltpu.SemaphoreType.DMA],
        compiler_params=PARAMS,
        name="brought_in",
    )(gram)


def per_device(test_grads, inverse_gram, train_grads):
    core = lax.axis_index("row") % CORE
    tests, width = test_grads.shape
    trains = train_grads.shape[0]
    half = tests // 2

    mine = jnp.where(core == 0, test_grads[:half], test_grads[half:])
    other = jnp.where(core == 0, test_grads[half:], test_grads[:half])
    got = send(other, TO_CORE)
    got, inverse_gram, train_grads = lax.optimization_barrier((got, inverse_gram, train_grads))
    far_gram = send(inverse_gram, TO_CORE)
    far_trains = send(train_grads, TO_CORE)

    block = jnp.concatenate([mine, got], axis=1)
    block = gather(block, FIRST).reshape(4 * half, 2 * width)
    near = brought_in(inverse_gram)
    block, near = lax.optimization_barrier((block, near))
    slot3, slot1 = send(block, SECOND[3]), send(block, SECOND[1])
    part = precond(jnp.concatenate([block, slot1]), near, far_gram)
    slot3, part = lax.optimization_barrier((slot3, part))
    slot2 = send(slot3, SECOND[1])

    def summed(part, e):
        part = part.reshape(Y, -1, part.shape[3])
        return scatter_sum([part[k] for k in range(Y)], TO_Y, e[:1])

    def rounded(total, e):
        return (total + unpack(send(pack(total, e), TO_ZH))[0]).astype(BF16)

    def product(low):
        scores, e = scores_of(low, train_grads, far_trains)
        scores = scores.reshape(2, 4 * half, 2 * trains)
        return [(scores[j], e[:1]) for j in range(2)]

    first = summed(*part)
    part = precond(jnp.concatenate([slot2, slot3]), near, far_gram)
    first, part = lax.optimization_barrier((first, part))
    second = summed(*part)
    low0 = rounded(*first)
    low1 = rounded(*second)
    low0 = gather(low0, TO_Y)
    low1 = gather(low1, TO_Y)
    block0, block1 = product(low0)
    block2, block3 = product(low1)
    total, least = block0
    for (block, e), k in ((block1, 1), (block3, 3), (block2, 2)):
        got, its = unpack(send(pack(block, e), SECOND[k]))
        total, least = total + got, jnp.minimum(least, its)
    total = total.reshape(4, half, 2 * trains)
    total, _ = scatter_sum([total[k] for k in range(4)], FIRST, least - 2.0, (3, 2, 1))

    kept, sent = total[:, :trains], total[:, trains:]
    got = send(sent, TO_CORE)
    return jnp.where(
        core == 0, jnp.concatenate([kept, got]), jnp.concatenate([got, kept])
    )


def solution(mesh):
    placed = (P("col", "row"), P("row", "col"), P("row", "col"))
    return jax.shard_map(
        per_device, mesh=mesh, in_specs=placed, out_specs=P("col", "row"), check_vma=False
    )
```
